32 devices in a mesh: sec: 4 (over z), blk: 8 (over y, x, core).
Axes of the slice: x: 2, y: 2, z: 4, core: 2. Of those that a mesh axis runs over, the one named last changes fastest.
Arguments:
- guess: bfloat16 [4, 8, 128, 8, 128], P('sec', None, None, 'blk'), may hold values from -6 to 6
- left_env: bfloat16 [4, 2, 8, 128, 128], P('sec', None, 'blk'), as said below
- right_env: bfloat16 [4, 2, 8, 128, 128], P('sec', None, 'blk'), as said below
- left_dims: int32 [4, 8], P('sec'), may hold values from 1 to 128, as said below
- right_dims: int32 [4, 8], P('sec'), may hold values from 1 to 128, as said below
- left_labels: int32 [4, 8], P('sec'), may hold values from 0 to 4, as said below
- right_labels: int32 [4, 8], P('sec'), may hold values from 0 to 4, as said below
Outputs:
- waves: float32 [4, 8, 128, 8, 128], P('sec', None, None, 'blk')
- energies: float32 [4, 2], P('sec')
The draws below stay inside these ranges and needn't reach their ends.
Inputs may be any that keep to these rules, and one draw needn't show every extreme that they name: `left_env`: every block of the environments is symmetric in its last two dimensions. `right_env`: every block of the environments is symmetric in its last two dimensions. `left_dims`: some sector of every section has all 128 states live. The left sectors of section s are the right sectors of section s - 1, with the same sizes. `right_dims`: some sector of every section has all 128 states live. `left_labels`: the left labels of section s are the right labels of section s - 1. Every particle number from 0 to 4 labels some sector of every bond. `right_labels`: every particle number from 0 to 4 labels some sector of every bond.
All inputs are finite; a program needn't handle non-finite values.
Results may differ from the reference program's by a relative error of at most 0.012.
Values may be sent and summed in bfloat16 or wider, within the bound.
A program may use at most 64 MiB of HBM per device.

```python
import jax
import jax.numpy as jnp
from jax import lax

BS = 128
W = 2
ITERS = 2
NSEC = 8
STATES = 1024
SECTIONS = 4


def symmetric_blocks(key):
    shape = (SECTIONS, W, NSEC, BS, BS)
    noise = jax.random.normal(key, shape, jnp.float32)
    return ((noise + jnp.swapaxes(noise, 3, 4)) * (0.5 / BS) ** 0.5).astype(jnp.bfloat16)


def boundary_ints(key):
    sizes_key = jax.random.fold_in(key, 101)
    position_key = jax.random.fold_in(key, 102)
    label_key = jax.random.fold_in(key, 103)
    sector_sizes = jax.random.randint(sizes_key, (SECTIONS + 1, NSEC), BS // 2, BS + 1)
    position = jax.random.randint(position_key, (SECTIONS + 1, 1), 0, NSEC)
    indices = jnp.arange(NSEC, dtype=jnp.int32)[None, :]
    sector_sizes = jnp.where(indices == position, BS, sector_sizes).astype(jnp.int32)
    label_keys = jax.random.split(label_key, SECTIONS + 1)
    orders = jax.vmap(lambda one_key: jax.random.permutation(one_key, NSEC))(label_keys)
    labels = (orders % 5).astype(jnp.int32)
    return (sector_sizes, labels)


def draw_left_env(key, part):
    return symmetric_blocks(jax.random.fold_in(key, 5))


def draw_right_env(key, part):
    return symmetric_blocks(jax.random.fold_in(key, 6))


def draw_left_dims(key, part):
    return boundary_ints(key)[0][:SECTIONS]


def draw_right_dims(key, part):
    return boundary_ints(key)[0][1:]


def draw_left_labels(key, part):
    return boundary_ints(key)[1][:SECTIONS]


def draw_right_labels(key, part):
    return boundary_ints(key)[1][1:]


def shard_levels(key, extent, cuts, low, largest):
    factor_of = 1.0
    for axis_at, parts in cuts:
        draws = jax.random.uniform(jax.random.fold_in(jax.random.fold_in(key, 6), axis_at), (parts,), jnp.float32, low / len(cuts), largest / len(cuts))
        factor_of = factor_of * jnp.repeat(jnp.exp(draws), extent[axis_at] // parts).reshape((-1,) + (1,) * (len(extent) - 1 - axis_at))
    return factor_of


def centred(stream_key, dims, deviation, reach, cuts=(), kind=jnp.bfloat16):
    array = deviation * jax.random.normal(stream_key, dims, jnp.float32)
    if cuts:
        array = array * shard_levels(stream_key, dims, cuts, -0.22, 0.18)
    return jnp.clip(array, -reach, reach).astype(kind)


def setup_inputs(seed: int = 0) -> dict:
    streams_of = jax.random.split(jax.random.key(seed), 8)
    guess = centred(streams_of[0], (SECTIONS, NSEC, BS, NSEC, BS), 1.0, 6.0, ((0, 4), (3, 8)))
    left_env = draw_left_env(jax.random.fold_in(streams_of[7], 71), 0)
    right_env = draw_right_env(jax.random.fold_in(streams_of[7], 71), 0)
    left_dims = draw_left_dims(jax.random.fold_in(streams_of[7], 71), 0)
    right_dims = draw_right_dims(jax.random.fold_in(streams_of[7], 71), 0)
    left_labels = draw_left_labels(jax.random.fold_in(streams_of[7], 71), 0)
    right_labels = draw_right_labels(jax.random.fold_in(streams_of[7], 71), 0)
    return {"guess": guess, "left_env": left_env, "right_env": right_env, "left_dims": left_dims, "right_dims": right_dims, "left_labels": left_labels, "right_labels": right_labels}


EPS = 1e-06

def block_mask(left_sizes, right_sizes, left_marks, right_marks, block_size):
    total = left_marks[:, None] + right_marks[None, :]
    allowed = (total == 4).astype(jnp.float32)
    offsets = jnp.arange(block_size, dtype=jnp.int32)
    live_rows = (offsets[None, :] < left_sizes[:, None]).astype(jnp.float32)
    live_cols = (offsets[None, :] < right_sizes[:, None]).astype(jnp.float32)
    return allowed[:, None, :, None] * live_rows[:, :, None, None] * live_cols[None, None, :, :]

def rounded_copy(vector):
    return lax.optimization_barrier(vector.astype(jnp.bfloat16)).astype(jnp.float32)

def left_product(rounded, left_block):
    return jnp.einsum('wqac,qcrb->wqarb', left_block.astype(jnp.float32), rounded).astype(jnp.bfloat16)

def hamiltonian(vector, left_block, right_block, pattern):
    left_done = left_product(rounded_copy(vector), left_block)
    return jnp.einsum('wqarc,wrbc->qarb', left_done.astype(jnp.float32), right_block.astype(jnp.float32)) * pattern

def davidson(start, left_block, right_block, pattern):
    vector = start.astype(jnp.float32) * pattern
    vector = vector / jnp.sqrt(jnp.sum(vector * vector) + EPS)
    image = hamiltonian(vector, left_block, right_block, pattern)
    ritz_value = jnp.sum(vector * image)
    for sweep in range(ITERS):
        residual = image - ritz_value * vector
        response = hamiltonian(residual, left_block, right_block, pattern)
        squared = jnp.sum(residual * residual) + EPS
        coupling = jnp.sum(residual * response) / squared
        midpoint = 0.5 * (ritz_value - coupling)
        radius = jnp.sqrt(midpoint * midpoint + squared)
        cosine = jnp.sqrt(0.5 * (1.0 - midpoint / radius))
        sine_value = -jnp.sqrt(0.5 * (1.0 + midpoint / radius))
        length = jnp.sqrt(squared)
        vector = cosine * vector + sine_value / length * residual
        image = cosine * image + sine_value / length * response
        ritz_value = 0.5 * (ritz_value + coupling) - radius
    return (vector, ritz_value)

def refresh(vector, left_block):
    rounded = rounded_copy(vector)
    left_done = left_product(rounded, left_block)
    return (STATES * jnp.einsum('qarb,wqarc->wrbc', rounded, left_done.astype(jnp.float32))).astype(jnp.bfloat16)

def reference(guess, left_env, right_env, left_dims, right_dims, left_labels, right_labels):
    first_vectors = []
    first_values = []
    freshes = []
    for section in range(SECTIONS):
        pattern = block_mask(left_dims[section], right_dims[section], left_labels[section], right_labels[section], BS)
        vector, value = davidson(guess[section], left_env[section], right_env[section], pattern)
        first_vectors.append(vector)
        first_values.append(value)
        freshes.append(refresh(vector, left_env[section]))
    waves = []
    energies = []
    for section in range(SECTIONS):
        pattern = block_mask(left_dims[section], right_dims[section], left_labels[section], right_labels[section], BS)
        if section == 0:
            second_left = left_env[0]
        else:
            second_left = freshes[section - 1]
        vector, value = davidson(first_vectors[section], second_left, right_env[section], pattern)
        waves.append(STATES * vector)
        energies.append(jnp.stack([first_values[section], value]))
    return (jnp.stack(waves), jnp.stack(energies))
```

```python
import functools

import jax
import jax.numpy as jnp
from jax import lax
from jax.experimental import pallas as pl
from jax.experimental.pallas import tpu as pltpu
from jax.sharding import PartitionSpec as P

MESH = pl.DeviceIdType.MESH
ITERS = 2
EPS = 1e-06
SPAN = 32.0
FLOOR = 1e-12
GROUP = 2


def partner(me, offset, count):
    if offset == 0:
        return me
    if count & (count - 1):
        return None
    result = 0
    bit = 1
    while bit < count:
        digit = lax.rem(lax.div(me, bit), 2)
        result = result + ((1 - digit) if offset & bit else digit) * bit
        bit *= 2
    return result


def target(me, offset, count):
    found = partner(me, offset, count)
    return lax.rem(me + offset, count) if found is None else found


def origin(me, offset, count):
    found = partner(me, offset, count)
    return lax.rem(me + count - offset, count) if found is None else found


def polynomial(mu, floor_squared):
    zero = jnp.zeros_like(mu[0])
    vector = [zero + 1.0]
    image = [zero, zero + 1.0]
    ritz = mu[1]
    for _ in range(ITERS):
        padded = vector + [zero]
        residual = [image[i] - ritz * padded[i] for i in range(len(image))]
        size = len(residual)
        squared = zero
        correlation = zero
        for i in range(size):
            for j in range(size):
                weight = residual[i] * residual[j]
                squared = squared + weight * mu[i + j]
                correlation = correlation + weight * mu[i + j + 1]
        squared = jnp.maximum(squared, 0.0) + floor_squared
        coupling = correlation / squared
        midpoint = 0.5 * (ritz - coupling)
        radius = jnp.sqrt(midpoint * midpoint + squared)
        cosine = jnp.sqrt(0.5 * (1.0 - midpoint / radius))
        sine = -jnp.sqrt(0.5 * (1.0 + midpoint / radius))
        tilt = sine / jnp.sqrt(squared)
        vector = [cosine * padded[i] + tilt * residual[i] for i in range(size)]
        image = [zero] + vector
        ritz = 0.5 * (ritz + coupling) - radius
    return vector, ritz


def kernel(
    count, sections, size, moments,
    left_dims, right_dims, left_labels, right_labels, guess_ref, left_ref, right_ref,
    waves_ref, energies_ref,
    guess, right, gathered, field, products, fresh, sums,
    local_sems, send_sems, recv_sems, pass_sems,
):
    sec = lax.axis_index("sec")
    me = lax.axis_index("blk")
    states = count * size
    has_next = sec < sections - 1
    has_previous = sec > 0

    load_right = pltpu.make_async_copy(right_ref, right, local_sems.at[0])
    load_left = pltpu.make_async_copy(left_ref, gathered.at[0, me], local_sems.at[1])
    load_guess = pltpu.make_async_copy(guess_ref, guess, local_sems.at[2])
    load_left.start()
    load_guess.start()
    load_right.start()

    barrier = pltpu.get_barrier_semaphore()
    for k in range(1, count):
        pl.semaphore_signal(barrier, inc=1, device_id=(sec, target(me, k, count)), device_id_type=MESH)

    @pl.when(has_next)
    def _():
        pl.semaphore_signal(barrier, inc=1, device_id=(sec + 1, me), device_id_type=MESH)

    @pl.when(has_previous)
    def _():
        pl.semaphore_signal(barrier, inc=1, device_id=(sec - 1, me), device_id_type=MESH)

    pl.semaphore_wait(barrier, count - 1 + has_next.astype(jnp.int32) + has_previous.astype(jnp.int32))

    def exchange(phase, source, slot):
        return {
            k: pltpu.make_async_remote_copy(
                src_ref=source,
                dst_ref=slot,
                send_sem=send_sems.at[phase, k],
                recv_sem=recv_sems.at[phase, k],
                device_id=(sec, target(me, k, count)),
                device_id_type=MESH,
            )
            for k in range(1, count)
        }

    first_copies = exchange(0, left_ref, gathered.at[0, me])
    for k in sorted(first_copies, reverse=True):
        first_copies[k].start()

    rows = lax.broadcasted_iota(jnp.int32, (size, size), 0)
    cols = lax.broadcasted_iota(jnp.int32, (size, size), 1)
    live_cols = cols < right_dims[0, me]
    mark = right_labels[0, me]

    def live(q):
        dims = jnp.where(left_labels[0, q] + mark == 4, left_dims[0, q], 0)
        return jnp.logical_and(rows < dims, live_cols)

    load_guess.wait()
    load_right.wait()
    right_all = right[...]
    right_peak = jnp.max(jnp.abs(right_all.astype(jnp.float32)), axis=(0, 1), keepdims=True) * SPAN

    def folded(values):
        return jnp.sum(values.reshape(-1, 8, size), axis=0)

    def chain(slot, qs, start):
        blocks = [gathered[slot, q] for q in qs]
        masks = [live(q) for q in qs]
        scales = [
            jnp.maximum(jnp.max(jnp.abs(b.astype(jnp.float32)), axis=(0, 1), keepdims=True) * right_peak, FLOOR)
            for b in blocks
        ]
        inverse = [1.0 / s for s in scales]
        powers = [[start(q, m) for q, m in zip(qs, masks)]]
        for _ in range(3):
            lefts = [
                jnp.dot(b, v.astype(jnp.bfloat16), preferred_element_type=jnp.float32).astype(jnp.bfloat16)
                for b, v in zip(blocks, powers[-1])
            ]
            lefts = [jnp.concatenate([t[:size], t[size:]], axis=1) for t in lefts]
            fulls = [jnp.dot(t, right_all, preferred_element_type=jnp.float32) for t in lefts]
            powers.append([jnp.where(m, f * i, 0.0) for m, f, i in zip(masks, fulls, inverse)])
        found = []
        for at, q in enumerate(qs):
            kept = [p[at] for p in powers]
            for i in range(3):
                field[i, q] = kept[i]
            found.append((scales[at], [folded(kept[i // 2] * kept[(i + 1) // 2]) for i in range(moments)]))
        return found

    def krylov(phase, slot, wait, start):
        found = []
        for first in range(0, count, GROUP):
            ks = range(first, min(first + GROUP, count))
            for k in ks:
                wait(k)
            found += chain(slot, [origin(me, k, count) for k in ks], start)
        peak = functools.reduce(jnp.maximum, [s for s, _ in found])
        totals = [None] * moments
        for scale, parts in found:
            ratio = scale / peak
            power = jnp.ones_like(ratio)
            for i in range(moments):
                term = parts[i] * power
                totals[i] = term if totals[i] is None else totals[i] + term
                power = power * ratio
        line = [jnp.sum(t, axis=0, keepdims=True) for t in totals]
        line.append(jnp.broadcast_to(peak, (1, size)))
        line.append(jnp.zeros((1, size), jnp.float32))
        row = phase // 2
        sums[row, me] = jnp.concatenate(line, axis=0)
        copies = exchange(phase, sums.at[row, me], sums.at[row, me])
        for k in copies:
            copies[k].start()
        for k in copies:
            copies[k].wait_recv()
        tiles = [sums[row, j] for j in range(count)]
        peaks = [t[moments : moments + 1] for t in tiles]
        top = functools.reduce(jnp.maximum, peaks)
        index = lax.broadcasted_iota(jnp.int32, (8, size), 0)
        total = jnp.zeros((8, size), jnp.float32)
        for tile, p in zip(tiles, peaks):
            ratio = p / top
            power = ratio
            weight = jnp.ones((8, size), jnp.float32)
            for i in range(1, moments):
                weight = jnp.where(index == i, power, weight)
                power = power * ratio
            total = total + tile * weight
        summed = jnp.broadcast_to(jnp.sum(total, axis=1, keepdims=True), (8, size))
        mu = [summed[i : i + 1] for i in range(moments)]
        norm = mu[0] + EPS
        mu = [m / norm for m in mu]
        relative = EPS**0.5 / top
        vector, ritz = polynomial(mu, relative * relative)
        shrink = lax.rsqrt(norm)
        weights = {}
        for k, (scale, _) in enumerate(found):
            ratio = scale / top
            weights[k] = [vector[0] * shrink, vector[1] * shrink * ratio, vector[2] * shrink * ratio * ratio]
        return weights, ritz * top, copies

    def combined(q, weight):
        return weight[0] * field[0, q] + weight[1] * field[1, q] + weight[2] * field[2, q]

    def wait_first(k):
        if k == 0:
            load_left.wait()
        else:
            first_copies[k].wait_recv()

    weights, first_ritz, first_sums = krylov(
        1, 0, wait_first, lambda q, m: jnp.where(m, guess[q].astype(jnp.float32), 0.0)
    )

    total = jnp.zeros((size, 2 * size), jnp.float32)
    for k in range(count):
        q = origin(me, k, count)
        vector = combined(q, weights[k])
        field[0, q] = vector
        rounded = vector.astype(jnp.bfloat16)
        done = jnp.dot(gathered[0, q], rounded, preferred_element_type=jnp.float32).astype(jnp.bfloat16)
        done = jnp.concatenate([done[:size], done[size:]], axis=1)
        total = total + lax.dot_general(
            rounded, done, (((0,), (0,)), ((), ())), preferred_element_type=jnp.float32
        )
    total = (states * total).astype(jnp.bfloat16)
    fresh[:size] = total[:, :size]
    fresh[size:] = total[:, size:]

    onward = pltpu.make_async_remote_copy(
        src_ref=fresh,
        dst_ref=gathered.at[1, me],
        send_sem=pass_sems.at[0],
        recv_sem=pass_sems.at[1],
        device_id=(lax.rem(sec + 1, sections), me),
        device_id_type=MESH,
    )

    @pl.when(has_next)
    def _():
        onward.start()

    second_copies = exchange(2, gathered.at[1, me], gathered.at[1, me])

    @pl.when(has_previous)
    def _():
        onward.wait_recv()
        for k in sorted(second_copies, reverse=True):
            second_copies[k].start()

    def wait_second(k):
        if k:

            @pl.when(has_previous)
            def _():
                second_copies[k].wait_recv()

    slot = jnp.where(has_previous, 1, 0)
    weights, second_ritz, second_sums = krylov(3, slot, wait_second, lambda q, m: field[0, q])

    for k in range(count):
        q = origin(me, k, count)
        waves_ref[q] = states * combined(q, weights[k])
    lane = lax.broadcasted_iota(jnp.int32, (1, size), 1)
    energies_ref[...] = jnp.where(lane == 0, first_ritz, second_ritz)[:, :2]

    for copies in (first_copies, first_sums, second_sums):
        for k in copies:
            copies[k].wait_send()

    @pl.when(has_previous)
    def _():
        for k in second_copies:
            second_copies[k].wait_send()

    @pl.when(has_next)
    def _():
        onward.wait_send()


def solution(mesh):
    count = mesh.shape["blk"]
    sections = mesh.shape["sec"]

    def local(guess, left_env, right_env, left_dims, right_dims, left_labels, right_labels):
        size = guess.shape[2]
        terms = left_env.shape[1]
        rows = terms * size
        smem = pl.BlockSpec(memory_space=pltpu.SMEM)
        anywhere = pl.BlockSpec(memory_space=pl.ANY)
        vmem = pl.BlockSpec(memory_space=pltpu.VMEM)
        moments = 2 * ITERS + 2
        waves, energies = pl.pallas_call(
            functools.partial(kernel, count, sections, size, moments),
            out_shape=(
                jax.ShapeDtypeStruct((count, size, size), jnp.float32),
                jax.ShapeDtypeStruct((1, 2), jnp.float32),
            ),
            in_specs=[smem] * 4 + [anywhere] * 3,
            out_specs=(vmem, vmem),
            scratch_shapes=[
                pltpu.VMEM((count, size, size), jnp.bfloat16),
                pltpu.VMEM((rows, size), jnp.bfloat16),
                pltpu.VMEM((2, count, rows, size), jnp.bfloat16),
                pltpu.VMEM((3, count, size, size), jnp.float32),
                pltpu.VMEM((8, size), jnp.float32),
                pltpu.VMEM((rows, size), jnp.bfloat16),
                pltpu.VMEM((2, count, 8, size), jnp.float32),
                pltpu.SemaphoreType.DMA((3,)),
                pltpu.SemaphoreType.DMA((4, count)),
                pltpu.SemaphoreType.DMA((4, count)),
                pltpu.SemaphoreType.DMA((2,)),
            ],
            compiler_params=pltpu.CompilerParams(
                collective_id=0, has_side_effects=True, vmem_limit_bytes=40 * 1024 * 1024
            ),
        )(
            left_dims, right_dims, left_labels, right_labels,
            guess.reshape(count, size, size), left_env.reshape(rows, size), right_env.reshape(rows, size),
        )
        return waves.reshape(1, count, size, 1, size), energies

    return jax.shard_map(
        local,
        mesh=mesh,
        in_specs=(
            P("sec", None, None, "blk", None),
            P("sec", None, "blk", None, None),
            P("sec", None, "blk", None, None),
            P("sec", None),
            P("sec", None),
            P("sec", None),
            P("sec", None),
        ),
        out_specs=(P("sec", None, None, "blk", None), P("sec", None)),
        check_vma=False,
    )
```

```python
import functools

import jax
import jax.numpy as jnp
from jax import lax
from jax.experimental import pallas as pl
from jax.experimental.pallas import tpu as pltpu
from jax.sharding import PartitionSpec as P

MESH = pl.DeviceIdType.MESH
ITERS = 2
EPS = 1e-06
SPAN = 32.0
FLOOR = 1e-12
GROUP = 4
TOTAL = 4


def target(me, offset, count):
    chip = lax.rem(lax.div(me, 2) + offset // 2, count // 2)
    return chip * 2 + lax.rem(me + offset, 2)


def origin(me, offset, count):
    chip = lax.rem(lax.div(me, 2) + count // 2 - offset // 2, count // 2)
    return chip * 2 + lax.rem(me + offset, 2)


def polynomial(mu, floor_squared):
    zero = jnp.zeros_like(mu[0])
    vector = [zero + 1.0]
    image = [zero, zero + 1.0]
    ritz = mu[1]
    for _ in range(ITERS):
        padded = vector + [zero]
        residual = [image[i] - ritz * padded[i] for i in range(len(image))]
        size = len(residual)
        squared = zero
        correlation = zero
        for i in range(size):
            for j in range(size):
                weight = residual[i] * residual[j]
                squared = squared + weight * mu[i + j]
                correlation = correlation + weight * mu[i + j + 1]
        squared = jnp.maximum(squared, 0.0) + floor_squared
        coupling = correlation / squared
        midpoint = 0.5 * (ritz - coupling)
        radius = jnp.sqrt(midpoint * midpoint + squared)
        cosine = jnp.sqrt(0.5 * (1.0 - midpoint / radius))
        sine = -jnp.sqrt(0.5 * (1.0 + midpoint / radius))
        tilt = sine / jnp.sqrt(squared)
        vector = [cosine * padded[i] + tilt * residual[i] for i in range(size)]
        image = [zero] + vector
        ritz = 0.5 * (ritz + coupling) - radius
    return vector, ritz


def kernel(
    count, sections, size, moments,
    left_dims, right_dims, left_labels, right_labels, guess_ref, left_ref, right_ref,
    waves_ref, energies_ref,
    guess, right, first_env, second_env, field, stats, fresh, sums, owner,
    local_sems, send_sems, recv_sems, pass_sems,
):
    sec = lax.axis_index("sec")
    me = lax.axis_index("blk")
    states = count * size
    slots = count - TOTAL
    has_next = sec < sections - 1
    has_previous = sec > 0

    load_left = pltpu.make_async_copy(left_ref, first_env.at[me], local_sems.at[1])
    load_guess = pltpu.make_async_copy(guess_ref, guess, local_sems.at[2])
    load_right = pltpu.make_async_copy(right_ref, right, local_sems.at[0])
    load_left.start()
    load_guess.start()
    load_right.start()

    barrier = pltpu.get_barrier_semaphore()
    for k in range(1, count):
        pl.semaphore_signal(barrier, inc=1, device_id=(sec, target(me, k, count)), device_id_type=MESH)

    @pl.when(has_next)
    def _():
        pl.semaphore_signal(barrier, inc=1, device_id=(sec + 1, me), device_id_type=MESH)

    @pl.when(has_previous)
    def _():
        pl.semaphore_signal(barrier, inc=1, device_id=(sec - 1, me), device_id_type=MESH)

    mark = right_labels[0, me]
    places = []
    seen = jnp.int32(0)
    matches = []
    for q in range(count):
        match = left_labels[0, q] + mark == TOTAL
        places.append(seen)
        matches.append(match)
        seen = seen + match.astype(jnp.int32)
    for t in range(slots):
        sector = jnp.int32(0)
        dims = jnp.int32(0)
        for q in range(count):
            here = jnp.logical_and(matches[q], places[q] == t)
            sector = jnp.where(here, q, sector)
            dims = jnp.where(here, left_dims[0, q], dims)
        owner[0, t] = sector
        owner[1, t] = dims

    load_left.wait()
    pl.semaphore_wait(barrier, count - 1 + has_next.astype(jnp.int32) + has_previous.astype(jnp.int32))

    def copy_to(phase, k, hop, source, slot):
        return pltpu.make_async_remote_copy(
            src_ref=source,
            dst_ref=slot,
            send_sem=send_sems.at[phase, k],
            recv_sem=recv_sems.at[phase, k],
            device_id=(sec, target(me, hop, count)),
            device_id_type=MESH,
        )

    def gather(phase, env):
        copies = {}
        for k in list(range(2, count, 2)) + [1]:
            copies[k] = copy_to(phase, k, k, env.at[me], env.at[me])
            copies[k].start()
        for k in range(2, count, 2):
            block = env.at[origin(me, k, count)]
            copies[k].wait_recv()
            copies[k + 1] = copy_to(phase, k + 1, 1, block, block)
            copies[k + 1].start()
        for k in range(1, count, 2):
            copies[k].wait_recv()
        for k in copies:
            copies[k].wait_send()

    gather(0, first_env)

    @pl.when(jnp.logical_not(has_previous))
    def _():
        pltpu.make_async_copy(first_env, second_env, local_sems.at[3]).start()

    rows = lax.broadcasted_iota(jnp.int32, (size, size), 0)
    cols = lax.broadcasted_iota(jnp.int32, (size, size), 1)
    live_cols = cols < right_dims[0, me]

    load_guess.wait()
    load_right.wait()
    right_all = right[...]
    right_peak = jnp.max(jnp.abs(right_all.astype(jnp.float32)), axis=(0, 1), keepdims=True) * SPAN

    def folded(values):
        return jnp.sum(values.reshape(-1, 8, size), axis=0)

    def chain(env, ts, start):
        sectors = [owner[0, t] for t in ts]
        blocks = [env[q] for q in sectors]
        masks = [jnp.logical_and(rows < owner[1, t], live_cols) for t in ts]
        scales = [
            jnp.maximum(jnp.max(jnp.abs(b.astype(jnp.float32)), axis=(0, 1), keepdims=True) * right_peak, FLOOR)
            for b in blocks
        ]
        inverse = [1.0 / s for s in scales]
        powers = [[start(t, q, m) for t, q, m in zip(ts, sectors, masks)]]
        for _ in range(3):
            lefts = [
                jnp.dot(b, v.astype(jnp.bfloat16), preferred_element_type=jnp.float32).astype(jnp.bfloat16)
                for b, v in zip(blocks, powers[-1])
            ]
            lefts = [jnp.concatenate([x[:size], x[size:]], axis=1) for x in lefts]
            full = jnp.dot(jnp.concatenate(lefts, axis=0), right_all, preferred_element_type=jnp.float32)
            powers.append([
                jnp.where(m, full[at * size : (at + 1) * size] * i, 0.0)
                for at, (m, i) in enumerate(zip(masks, inverse))
            ])
        for at, t in enumerate(ts):
            kept = [p[at] for p in powers]
            for i in range(3):
                field[i, t] = kept[i]
            line = [
                jnp.sum(folded(kept[i // 2] * kept[(i + 1) // 2]), axis=0, keepdims=True) for i in range(moments)
            ]
            line.append(jnp.broadcast_to(scales[at], (1, size)))
            line.append(jnp.zeros((1, size), jnp.float32))
            stats[t] = jnp.concatenate(line, axis=0)

    index = lax.broadcasted_iota(jnp.int32, (8, size), 0)

    def merged(tiles):
        peaks = [tile[moments : moments + 1] for tile in tiles]
        top = functools.reduce(jnp.maximum, peaks)
        total = jnp.zeros((8, size), jnp.float32)
        for tile, peak in zip(tiles, peaks):
            ratio = peak / top
            power = ratio
            weight = jnp.ones((8, size), jnp.float32)
            for i in range(1, moments):
                weight = jnp.where(index == i, power, weight)
                power = power * ratio
            total = total + tile * weight
        return jnp.where(index == moments, top, total), top

    def krylov(phase, env, start):
        if slots % GROUP == 0 and slots > GROUP:

            def step(g, carry):
                chain(env, [g * GROUP + i for i in range(GROUP)], start)
                return carry

            lax.fori_loop(0, slots // GROUP, step, 0)
        else:
            for first in range(0, slots, GROUP):
                chain(env, list(range(first, min(first + GROUP, slots))), start)
        row = phase // 2
        tiles = [stats[t] for t in range(slots)]
        sums[row, me] = merged(tiles)[0]
        copies = {k: copy_to(phase, k, k, sums.at[row, me], sums.at[row, me]) for k in range(1, count)}
        for k in copies:
            copies[k].start()
        for k in copies:
            copies[k].wait_recv()
        total, top = merged([sums[row, j] for j in range(count)])
        summed = jnp.broadcast_to(jnp.sum(total, axis=1, keepdims=True), (8, size))
        mu = [summed[i : i + 1] for i in range(moments)]
        norm = mu[0] + EPS
        mu = [m / norm for m in mu]
        relative = EPS**0.5 / top
        vector, ritz = polynomial(mu, relative * relative)
        shrink = lax.rsqrt(norm)
        weights = []
        for tile in tiles:
            ratio = tile[moments : moments + 1] / top
            weights.append([vector[0] * shrink, vector[1] * shrink * ratio, vector[2] * shrink * ratio * ratio])
        return weights, ritz * top, copies

    def combined(t, weight):
        return weight[0] * field[0, t] + weight[1] * field[1, t] + weight[2] * field[2, t]

    weights, first_ritz, first_sums = krylov(
        1, first_env, lambda t, q, m: jnp.where(m, guess[q].astype(jnp.float32), 0.0)
    )

    total = jnp.zeros((size, 2 * size), jnp.float32)
    for t in range(slots):
        vector = combined(t, weights[t])
        field[0, t] = vector
        rounded = vector.astype(jnp.bfloat16)
        done = jnp.dot(first_env[owner[0, t]], rounded, preferred_element_type=jnp.float32).astype(jnp.bfloat16)
        done = jnp.concatenate([done[:size], done[size:]], axis=1)
        total = total + lax.dot_general(
            rounded, done, (((0,), (0,)), ((), ())), preferred_element_type=jnp.float32
        )
    total = (states * total).astype(jnp.bfloat16)
    fresh[:size] = total[:, :size]
    fresh[size:] = total[:, size:]

    onward = pltpu.make_async_remote_copy(
        src_ref=fresh,
        dst_ref=second_env.at[me],
        send_sem=pass_sems.at[0],
        recv_sem=pass_sems.at[1],
        device_id=(lax.rem(sec + 1, sections), me),
        device_id_type=MESH,
    )

    @pl.when(has_next)
    def _():
        onward.start()

    @pl.when(has_previous)
    def _():
        onward.wait_recv()
        gather(2, second_env)

    @pl.when(jnp.logical_not(has_previous))
    def _():
        pltpu.make_async_copy(first_env, second_env, local_sems.at[3]).wait()

    weights, second_ritz, second_sums = krylov(3, second_env, lambda t, q, m: field[0, t])

    for t in range(slots):
        field[0, t] = states * combined(t, weights[t])
    for q in range(count):
        waves_ref[q] = jnp.where(matches[q], field[0, jnp.minimum(places[q], slots - 1)], 0.0)
    lane = lax.broadcasted_iota(jnp.int32, (1, size), 1)
    energies_ref[...] = jnp.where(lane == 0, first_ritz, second_ritz)[:, :2]

    for copies in (first_sums, second_sums):
        for k in copies:
            copies[k].wait_send()

    @pl.when(has_next)
    def _():
        onward.wait_send()


def solution(mesh):
    count = mesh.shape["blk"]
    sections = mesh.shape["sec"]

    def local(guess, left_env, right_env, left_dims, right_dims, left_labels, right_labels):
        size = guess.shape[2]
        terms = left_env.shape[1]
        rows = terms * size
        smem = pl.BlockSpec(memory_space=pltpu.SMEM)
        anywhere = pl.BlockSpec(memory_space=pltpu.HBM)
        vmem = pl.BlockSpec(memory_space=pltpu.VMEM)
        moments = 2 * ITERS + 2
        waves, energies = pl.pallas_call(
            functools.partial(kernel, count, sections, size, moments),
            out_shape=(
                jax.ShapeDtypeStruct((count, size, size), jnp.float32),
                jax.ShapeDtypeStruct((1, 2), jnp.float32),
            ),
            in_specs=[smem] * 4 + [anywhere] * 3,
            out_specs=(vmem, vmem),
            scratch_shapes=[
                pltpu.VMEM((count, size, size), jnp.bfloat16),
                pltpu.VMEM((rows, size), jnp.bfloat16),
                pltpu.VMEM((count, rows, size), jnp.bfloat16),
                pltpu.VMEM((count, rows, size), jnp.bfloat16),
                pltpu.VMEM((3, count - TOTAL, size, size), jnp.float32),
                pltpu.VMEM((count - TOTAL, 8, size), jnp.float32),
                pltpu.VMEM((rows, size), jnp.bfloat16),
                pltpu.VMEM((2, count, 8, size), jnp.float32),
                pltpu.SMEM((2, count), jnp.int32),
                pltpu.SemaphoreType.DMA((4,)),
                pltpu.SemaphoreType.DMA((4, count)),
                pltpu.SemaphoreType.DMA((4, count)),
                pltpu.SemaphoreType.DMA((2,)),
            ],
            compiler_params=pltpu.CompilerParams(
                collective_id=0, has_side_effects=True, vmem_limit_bytes=64800 * 1024
            ),
        )(
            left_dims, right_dims, left_labels, right_labels,
            guess.reshape(count, size, size), left_env.reshape(rows, size), right_env.reshape(rows, size),
        )
        return waves.reshape(1, count, size, 1, size), energies

    return jax.shard_map(
        local,
        mesh=mesh,
        in_specs=(
            P("sec", None, None, "blk", None),
            P("sec", None, "blk", None, None),
            P("sec", None, "blk", None, None),
            P("sec", None),
            P("sec", None),
            P("sec", None),
            P("sec", None),
        ),
        out_specs=(P("sec", None, None, "blk", None), P("sec", None)),
        check_vma=False,
    )
```

```python
import functools

import jax
import jax.numpy as jnp
from jax import lax
from jax.experimental import pallas as pl
from jax.experimental.pallas import tpu as pltpu
from jax.sharding import PartitionSpec as P

MESH = pl.DeviceIdType.MESH
ITERS = 2
EPS = 1e-06
SPAN = 32.0
FLOOR = 1e-12
GROUP = 4
TOTAL = 4
TERMS = 2


def target(me, offset, count):
    chip = lax.rem(lax.div(me, 2) + offset // 2, count // 2)
    return chip * 2 + lax.rem(me + offset, 2)


def origin(me, offset, count):
    chip = lax.rem(lax.div(me, 2) + count // 2 - offset // 2, count // 2)
    return chip * 2 + lax.rem(me + offset, 2)


def polynomial(mu, floor_squared):
    zero = jnp.zeros_like(mu[0])
    vector = [zero + 1.0]
    image = [zero, zero + 1.0]
    ritz = mu[1]
    for _ in range(ITERS):
        padded = vector + [zero]
        residual = [image[i] - ritz * padded[i] for i in range(len(image))]
        size = len(residual)
        squared = zero
        correlation = zero
        for i in range(size):
            for j in range(size):
                weight = residual[i] * residual[j]
                squared = squared + weight * mu[i + j]
                correlation = correlation + weight * mu[i + j + 1]
        squared = jnp.maximum(squared, 0.0) + floor_squared
        coupling = correlation / squared
        midpoint = 0.5 * (ritz - coupling)
        radius = jnp.sqrt(midpoint * midpoint + squared)
        cosine = jnp.sqrt(0.5 * (1.0 - midpoint / radius))
        sine = -jnp.sqrt(0.5 * (1.0 + midpoint / radius))
        tilt = sine / jnp.sqrt(squared)
        vector = [cosine * padded[i] + tilt * residual[i] for i in range(size)]
        image = [zero] + vector
        ritz = 0.5 * (ritz + coupling) - radius
    return vector, ritz


def kernel(
    count, sections, size, moments,
    left_dims, right_dims, left_labels, right_labels, guess_ref, left_ref, right_ref,
    waves_ref, energies_ref,
    guess, right, first_env, second_env, field, stats, fresh, sums, owner,
    local_sems, send_sems, recv_sems, pass_sems,
):
    sec = lax.axis_index("sec")
    me = lax.axis_index("blk")
    states = count * size
    slots = count - TOTAL
    has_next = sec < sections - 1
    has_previous = sec > 0

    load_left = pltpu.make_async_copy(left_ref, first_env.at[me], local_sems.at[1])
    load_guess = pltpu.make_async_copy(guess_ref, guess, local_sems.at[2])
    load_right = pltpu.make_async_copy(right_ref, right, local_sems.at[0])
    load_left.start()
    load_guess.start()
    load_right.start()

    barrier = pltpu.get_barrier_semaphore()
    for k in range(1, count):
        pl.semaphore_signal(barrier, inc=1, device_id=(sec, target(me, k, count)), device_id_type=MESH)

    @pl.when(has_next)
    def _():
        pl.semaphore_signal(barrier, inc=1, device_id=(sec + 1, me), device_id_type=MESH)

    @pl.when(has_previous)
    def _():
        pl.semaphore_signal(barrier, inc=1, device_id=(sec - 1, me), device_id_type=MESH)

    mark = right_labels[0, me]
    places = []
    seen = jnp.int32(0)
    matches = []
    for q in range(count):
        match = left_labels[0, q] + mark == TOTAL
        places.append(seen)
        matches.append(match)
        seen = seen + match.astype(jnp.int32)
    for t in range(slots):
        sector = jnp.int32(0)
        dims = jnp.int32(0)
        for q in range(count):
            here = jnp.logical_and(matches[q], places[q] == t)
            sector = jnp.where(here, q, sector)
            dims = jnp.where(here, left_dims[0, q], dims)
        owner[0, t] = sector
        owner[1, t] = dims

    load_left.wait()
    pl.semaphore_wait(barrier, count - 1 + has_next.astype(jnp.int32) + has_previous.astype(jnp.int32))

    def copy_to(phase, k, hop, source, slot, part=0):
        return pltpu.make_async_remote_copy(
            src_ref=source,
            dst_ref=slot,
            send_sem=send_sems.at[phase, k, part],
            recv_sem=recv_sems.at[phase, k, part],
            device_id=(sec, target(me, hop, count)),
            device_id_type=MESH,
        )

    def term(ref, w):
        return ref.at[pl.ds(w * size, size)]

    def gather(phase, env, arrive):
        copies = {}
        for w in range(TERMS):
            arrive(w)
            block = term(env.at[me], w)
            for k in list(range(2, count, 2)) + [1]:
                copies[k, w] = copy_to(phase, k, k, block, block, w)
                copies[k, w].start()
        for w in range(TERMS):
            for k in range(2, count, 2):
                block = term(env.at[origin(me, k, count)], w)
                copies[k, w].wait_recv()
                copies[k + 1, w] = copy_to(phase, k + 1, 1, block, block, w)
                copies[k + 1, w].start()
        for w in range(TERMS):
            for k in range(1, count, 2):
                copies[k, w].wait_recv()
        for key in copies:
            copies[key].wait_send()

    gather(0, first_env, lambda w: None)

    @pl.when(jnp.logical_not(has_previous))
    def _():
        pltpu.make_async_copy(first_env, second_env, local_sems.at[3]).start()

    rows = lax.broadcasted_iota(jnp.int32, (size, size), 0)
    cols = lax.broadcasted_iota(jnp.int32, (size, size), 1)
    live_cols = cols < right_dims[0, me]

    load_guess.wait()
    load_right.wait()
    right_all = right[...]
    right_peak = jnp.max(jnp.abs(right_all.astype(jnp.float32)), axis=(0, 1), keepdims=True) * SPAN

    def folded(values):
        return jnp.sum(values.reshape(-1, 8, size), axis=0)

    def chain(env, ts, start):
        sectors = [owner[0, t] for t in ts]
        blocks = [env[q] for q in sectors]
        masks = [jnp.logical_and(rows < owner[1, t], live_cols) for t in ts]
        scales = [
            jnp.maximum(jnp.max(jnp.abs(b.astype(jnp.float32)), axis=(0, 1), keepdims=True) * right_peak, FLOOR)
            for b in blocks
        ]
        inverse = [1.0 / s for s in scales]
        powers = [[start(t, q, m) for t, q, m in zip(ts, sectors, masks)]]
        for _ in range(3):
            lefts = [
                jnp.dot(b, v.astype(jnp.bfloat16), preferred_element_type=jnp.float32).astype(jnp.bfloat16)
                for b, v in zip(blocks, powers[-1])
            ]
            lefts = [jnp.concatenate([x[:size], x[size:]], axis=1) for x in lefts]
            full = jnp.dot(jnp.concatenate(lefts, axis=0), right_all, preferred_element_type=jnp.float32)
            powers.append([
                jnp.where(m, full[at * size : (at + 1) * size] * i, 0.0)
                for at, (m, i) in enumerate(zip(masks, inverse))
            ])
        for at, t in enumerate(ts):
            kept = [p[at] for p in powers]
            for i in range(3):
                field[i, t] = kept[i]
            line = [
                jnp.sum(folded(kept[i // 2] * kept[(i + 1) // 2]), axis=0, keepdims=True) for i in range(moments)
            ]
            line.append(jnp.broadcast_to(scales[at], (1, size)))
            line.append(jnp.zeros((1, size), jnp.float32))
            stats[t] = jnp.concatenate(line, axis=0)

    index = lax.broadcasted_iota(jnp.int32, (8, size), 0)

    def merged(tiles):
        peaks = [tile[moments : moments + 1] for tile in tiles]
        top = functools.reduce(jnp.maximum, peaks)
        total = jnp.zeros((8, size), jnp.float32)
        for tile, peak in zip(tiles, peaks):
            ratio = peak / top
            power = ratio
            weight = jnp.ones((8, size), jnp.float32)
            for i in range(1, moments):
                weight = jnp.where(index == i, power, weight)
                power = power * ratio
            total = total + tile * weight
        return jnp.where(index == moments, top, total), top

    def krylov(phase, env, start):
        if slots % GROUP == 0 and slots > GROUP:

            def step(g, carry):
                chain(env, [g * GROUP + i for i in range(GROUP)], start)
                return carry

            lax.fori_loop(0, slots // GROUP, step, 0)
        else:
            for first in range(0, slots, GROUP):
                chain(env, list(range(first, min(first + GROUP, slots))), start)
        row = phase // 2
        tiles = [stats[t] for t in range(slots)]
        sums[row, me] = merged(tiles)[0]
        copies = {k: copy_to(phase, k, k, sums.at[row, me], sums.at[row, me]) for k in range(1, count)}
        for k in copies:
            copies[k].start()
        for k in copies:
            copies[k].wait_recv()
        total, top = merged([sums[row, j] for j in range(count)])
        summed = jnp.broadcast_to(jnp.sum(total, axis=1, keepdims=True), (8, size))
        mu = [summed[i : i + 1] for i in range(moments)]
        norm = mu[0] + EPS
        mu = [m / norm for m in mu]
        relative = EPS**0.5 / top
        vector, ritz = polynomial(mu, relative * relative)
        shrink = lax.rsqrt(norm)
        weights = []
        for tile in tiles:
            ratio = tile[moments : moments + 1] / top
            weights.append([vector[0] * shrink, vector[1] * shrink * ratio, vector[2] * shrink * ratio * ratio])
        return weights, ritz * top, copies

    def combined(t, weight):
        return weight[0] * field[0, t] + weight[1] * field[1, t] + weight[2] * field[2, t]

    weights, first_ritz, first_sums = krylov(
        1, first_env, lambda t, q, m: jnp.where(m, guess[q].astype(jnp.float32), 0.0)
    )

    onward = [
        pltpu.make_async_remote_copy(
            src_ref=term(fresh, w),
            dst_ref=term(second_env.at[me], w),
            send_sem=pass_sems.at[0, w],
            recv_sem=pass_sems.at[1, w],
            device_id=(lax.rem(sec + 1, sections), me),
            device_id_type=MESH,
        )
        for w in range(TERMS)
    ]
    rounded = []
    for t in range(slots):
        vector = combined(t, weights[t])
        field[0, t] = vector
        rounded.append(vector.astype(jnp.bfloat16))
    for w in range(TERMS):
        total = jnp.zeros((size, size), jnp.float32)
        for t in range(slots):
            block = first_env[owner[0, t], w * size : (w + 1) * size]
            done = jnp.dot(block, rounded[t], preferred_element_type=jnp.float32).astype(jnp.bfloat16)
            total = total + lax.dot_general(
                rounded[t], done, (((0,), (0,)), ((), ())), preferred_element_type=jnp.float32
            )
        fresh[w * size : (w + 1) * size] = (states * total).astype(jnp.bfloat16)

        @pl.when(has_next)
        def _(w=w):
            onward[w].start()

    @pl.when(has_previous)
    def _():
        gather(2, second_env, lambda w: onward[w].wait_recv())

    @pl.when(jnp.logical_not(has_previous))
    def _():
        pltpu.make_async_copy(first_env, second_env, local_sems.at[3]).wait()

    weights, second_ritz, second_sums = krylov(3, second_env, lambda t, q, m: field[0, t])

    for t in range(slots):
        field[0, t] = states * combined(t, weights[t])
    for q in range(count):
        waves_ref[q] = jnp.where(matches[q], field[0, jnp.minimum(places[q], slots - 1)], 0.0)
    lane = lax.broadcasted_iota(jnp.int32, (1, size), 1)
    energies_ref[...] = jnp.where(lane == 0, first_ritz, second_ritz)[:, :2]

    for copies in (first_sums, second_sums):
        for k in copies:
            copies[k].wait_send()

    @pl.when(has_next)
    def _():
        for copy in onward:
            copy.wait_send()


def solution(mesh):
    count = mesh.shape["blk"]
    sections = mesh.shape["sec"]

    def local(guess, left_env, right_env, left_dims, right_dims, left_labels, right_labels):
        size = guess.shape[2]
        terms = left_env.shape[1]
        rows = terms * size
        smem = pl.BlockSpec(memory_space=pltpu.SMEM)
        anywhere = pl.BlockSpec(memory_space=pltpu.HBM)
        vmem = pl.BlockSpec(memory_space=pltpu.VMEM)
        moments = 2 * ITERS + 2
        waves, energies = pl.pallas_call(
            functools.partial(kernel, count, sections, size, moments),
            out_shape=(
                pltpu.VMEM((count, size, size), jnp.float32),
                pltpu.VMEM((1, 2), jnp.float32),
            ),
            in_specs=[smem] * 4 + [anywhere] * 3,
            out_specs=(vmem, vmem),
            scratch_shapes=[
                pltpu.VMEM((count, size, size), jnp.bfloat16),
                pltpu.VMEM((rows, size), jnp.bfloat16),
                pltpu.VMEM((count, rows, size), jnp.bfloat16),
                pltpu.VMEM((count, rows, size), jnp.bfloat16),
                pltpu.VMEM((3, count - TOTAL, size, size), jnp.float32),
                pltpu.VMEM((count - TOTAL, 8, size), jnp.float32),
                pltpu.VMEM((rows, size), jnp.bfloat16),
                pltpu.VMEM((2, count, 8, size), jnp.float32),
                pltpu.SMEM((2, count), jnp.int32),
                pltpu.SemaphoreType.DMA((4,)),
                pltpu.SemaphoreType.DMA((4, count, TERMS)),
                pltpu.SemaphoreType.DMA((4, count, TERMS)),
                pltpu.SemaphoreType.DMA((2, TERMS)),
            ],
            compiler_params=pltpu.CompilerParams(
                collective_id=0, has_side_effects=True, vmem_limit_bytes=64 * 1024 * 1024 - 10 * count * size * size
            ),
        )(
            left_dims, right_dims, left_labels, right_labels,
            guess.reshape(count, size, size), left_env.reshape(rows, size), right_env.reshape(rows, size),
        )
        return waves.reshape(1, count, size, 1, size), energies

    return jax.shard_map(
        local,
        mesh=mesh,
        in_specs=(
            P("sec", None, None, "blk", None),
            P("sec", None, "blk", None, None),
            P("sec", None, "blk", None, None),
            P("sec", None),
            P("sec", None),
            P("sec", None),
            P("sec", None),
        ),
        out_specs=(P("sec", None, None, "blk", None), P("sec", None)),
        check_vma=False,
    )
```

```python
import functools

import jax
import jax.numpy as jnp
from jax import lax
from jax.experimental import pallas as pl
from jax.experimental.pallas import tpu as pltpu
from jax.sharding import PartitionSpec as P

MESH = pl.DeviceIdType.MESH
ITERS = 2
EPS = 1e-06
SPAN = 32.0
FLOOR = 1e-12
GROUP = 4
TOTAL = 4
TERMS = 2


def target(me, offset, count):
    chip = lax.rem(lax.div(me, 2) + offset // 2, count // 2)
    return chip * 2 + lax.rem(me + offset, 2)


def origin(me, offset, count):
    chip = lax.rem(lax.div(me, 2) + count // 2 - offset // 2, count // 2)
    return chip * 2 + lax.rem(me + offset, 2)


def polynomial(mu, floor_squared):
    zero = jnp.zeros_like(mu[0])
    vector = [zero + 1.0]
    image = [zero, zero + 1.0]
    ritz = mu[1]
    for _ in range(ITERS):
        padded = vector + [zero]
        residual = [image[i] - ritz * padded[i] for i in range(len(image))]
        size = len(residual)
        squared = zero
        correlation = zero
        for i in range(size):
            for j in range(size):
                weight = residual[i] * residual[j]
                squared = squared + weight * mu[i + j]
                correlation = correlation + weight * mu[i + j + 1]
        squared = jnp.maximum(squared, 0.0) + floor_squared
        coupling = correlation / squared
        midpoint = 0.5 * (ritz - coupling)
        radius = jnp.sqrt(midpoint * midpoint + squared)
        cosine = jnp.sqrt(0.5 * (1.0 - midpoint / radius))
        sine = -jnp.sqrt(0.5 * (1.0 + midpoint / radius))
        tilt = sine / jnp.sqrt(squared)
        vector = [cosine * padded[i] + tilt * residual[i] for i in range(size)]
        image = [zero] + vector
        ritz = 0.5 * (ritz + coupling) - radius
    return vector, ritz


def kernel(
    count, sections, size, moments,
    left_dims, right_dims, left_labels, right_labels, guess_ref, left_ref, right_ref,
    waves_ref, energies_ref,
    guess, right, first_env, second_env, field, stats, fresh, sums, owner,
    local_sems, send_sems, recv_sems, pass_sems,
):
    sec = lax.axis_index("sec")
    me = lax.axis_index("blk")
    states = count * size
    slots = count - TOTAL
    has_next = sec < sections - 1
    has_previous = sec > 0

    load_left = pltpu.make_async_copy(left_ref, first_env.at[me], local_sems.at[1])
    load_guess = pltpu.make_async_copy(guess_ref, guess, local_sems.at[2])
    load_right = pltpu.make_async_copy(right_ref, right, local_sems.at[0])
    load_left.start()
    load_guess.start()
    load_right.start()

    barrier = pltpu.get_barrier_semaphore()
    for k in range(1, count):
        pl.semaphore_signal(barrier, inc=1, device_id=(sec, target(me, k, count)), device_id_type=MESH)

    @pl.when(has_next)
    def _():
        pl.semaphore_signal(barrier, inc=1, device_id=(sec + 1, me), device_id_type=MESH)

    @pl.when(has_previous)
    def _():
        pl.semaphore_signal(barrier, inc=1, device_id=(sec - 1, me), device_id_type=MESH)

    mark = right_labels[0, me]
    places = []
    seen = jnp.int32(0)
    matches = []
    for q in range(count):
        match = left_labels[0, q] + mark == TOTAL
        places.append(seen)
        matches.append(match)
        seen = seen + match.astype(jnp.int32)
    for t in range(slots):
        sector = jnp.int32(0)
        dims = jnp.int32(0)
        for q in range(count):
            here = jnp.logical_and(matches[q], places[q] == t)
            sector = jnp.where(here, q, sector)
            dims = jnp.where(here, left_dims[0, q], dims)
        owner[0, t] = sector
        owner[1, t] = dims

    load_left.wait()
    pl.semaphore_wait(barrier, count - 1 + has_next.astype(jnp.int32) + has_previous.astype(jnp.int32))

    def copy_to(phase, k, hop, source, slot, part=0):
        return pltpu.make_async_remote_copy(
            src_ref=source,
            dst_ref=slot,
            send_sem=send_sems.at[phase, k, part],
            recv_sem=recv_sems.at[phase, k, part],
            device_id=(sec, target(me, hop, count)),
            device_id_type=MESH,
        )

    def term(ref, w):
        return ref.at[pl.ds(w * size, size)]

    def gather(phase, env, arrive):
        copies = {}
        for w in range(TERMS):
            arrive(w)
            block = term(env.at[me], w)
            for k in list(range(count - 2, 0, -2)) + [1]:
                copies[k, w] = copy_to(phase, k, k, block, block, w)
                copies[k, w].start()
        for w in range(TERMS):
            for k in range(2, count, 2):
                block = term(env.at[origin(me, k, count)], w)
                copies[k, w].wait_recv()
                copies[k + 1, w] = copy_to(phase, k + 1, 1, block, block, w)
                copies[k + 1, w].start()
        for w in range(TERMS):
            for k in range(1, count, 2):
                copies[k, w].wait_recv()
        return copies.values()

    first_copies = gather(0, first_env, lambda w: None)

    @pl.when(jnp.logical_not(has_previous))
    def _():
        pltpu.make_async_copy(first_env, second_env, local_sems.at[3]).start()

    rows = lax.broadcasted_iota(jnp.int32, (size, size), 0)
    cols = lax.broadcasted_iota(jnp.int32, (size, size), 1)
    live_cols = cols < right_dims[0, me]

    load_guess.wait()
    load_right.wait()
    right_all = right[...]
    right_peak = jnp.max(jnp.abs(right_all.astype(jnp.float32)), axis=(0, 1), keepdims=True) * SPAN

    def folded(values):
        return jnp.sum(values.reshape(-1, 8, size), axis=0)

    def chain(env, ts, start):
        sectors = [owner[0, t] for t in ts]
        blocks = [env[q] for q in sectors]
        masks = [jnp.logical_and(rows < owner[1, t], live_cols) for t in ts]
        scales = [
            jnp.maximum(jnp.max(jnp.abs(b.astype(jnp.float32)), axis=(0, 1), keepdims=True) * right_peak, FLOOR)
            for b in blocks
        ]
        inverse = [1.0 / s for s in scales]
        powers = [[start(t, q, m) for t, q, m in zip(ts, sectors, masks)]]
        for _ in range(3):
            lefts = [
                jnp.dot(b, v.astype(jnp.bfloat16), preferred_element_type=jnp.float32).astype(jnp.bfloat16)
                for b, v in zip(blocks, powers[-1])
            ]
            lefts = [jnp.concatenate([x[:size], x[size:]], axis=1) for x in lefts]
            full = jnp.dot(jnp.concatenate(lefts, axis=0), right_all, preferred_element_type=jnp.float32)
            powers.append([
                jnp.where(m, full[at * size : (at + 1) * size] * i, 0.0)
                for at, (m, i) in enumerate(zip(masks, inverse))
            ])
        for at, t in enumerate(ts):
            kept = [p[at] for p in powers]
            for i in range(3):
                field[i, t] = kept[i]
            line = [
                jnp.sum(folded(kept[i // 2] * kept[(i + 1) // 2]), axis=0, keepdims=True) for i in range(moments)
            ]
            line.append(jnp.broadcast_to(scales[at], (1, size)))
            line.append(jnp.zeros((1, size), jnp.float32))
            stats[t] = jnp.concatenate(line, axis=0)

    index = lax.broadcasted_iota(jnp.int32, (8, size), 0)

    def merged(tiles):
        peaks = [tile[moments : moments + 1] for tile in tiles]
        top = functools.reduce(jnp.maximum, peaks)
        total = jnp.zeros((8, size), jnp.float32)
        for tile, peak in zip(tiles, peaks):
            ratio = peak / top
            power = ratio
            weight = jnp.ones((8, size), jnp.float32)
            for i in range(1, moments):
                weight = jnp.where(index == i, power, weight)
                power = power * ratio
            total = total + tile * weight
        return jnp.where(index == moments, top, total), top

    def krylov(phase, env, start):
        if slots % GROUP == 0 and slots > GROUP:

            def step(g, carry):
                chain(env, [g * GROUP + i for i in range(GROUP)], start)
                return carry

            lax.fori_loop(0, slots // GROUP, step, 0)
        else:
            for first in range(0, slots, GROUP):
                chain(env, list(range(first, min(first + GROUP, slots))), start)
        row = phase // 2
        tiles = [stats[t] for t in range(slots)]
        sums[row, me] = merged(tiles)[0]
        copies = {k: copy_to(phase, k, k, sums.at[row, me], sums.at[row, me]) for k in range(1, count)}
        for k in copies:
            copies[k].start()
        for k in copies:
            copies[k].wait_recv()
        total, top = merged([sums[row, j] for j in range(count)])
        summed = jnp.broadcast_to(jnp.sum(total, axis=1, keepdims=True), (8, size))
        mu = [summed[i : i + 1] for i in range(moments)]
        norm = mu[0] + EPS
        mu = [m / norm for m in mu]
        relative = EPS**0.5 / top
        vector, ritz = polynomial(mu, relative * relative)
        shrink = lax.rsqrt(norm)
        weights = []
        for tile in tiles:
            ratio = tile[moments : moments + 1] / top
            weights.append([vector[0] * shrink, vector[1] * shrink * ratio, vector[2] * shrink * ratio * ratio])
        return weights, ritz * top, copies

    def combined(t, weight):
        return weight[0] * field[0, t] + weight[1] * field[1, t] + weight[2] * field[2, t]

    weights, first_ritz, first_sums = krylov(
        1, first_env, lambda t, q, m: jnp.where(m, guess[q].astype(jnp.float32), 0.0)
    )

    onward = [
        pltpu.make_async_remote_copy(
            src_ref=term(fresh, w),
            dst_ref=term(second_env.at[me], w),
            send_sem=pass_sems.at[0, w],
            recv_sem=pass_sems.at[1, w],
            device_id=(lax.rem(sec + 1, sections), me),
            device_id_type=MESH,
        )
        for w in range(TERMS)
    ]
    rounded = []
    for t in range(slots):
        vector = combined(t, weights[t])
        field[0, t] = vector
        rounded.append(vector.astype(jnp.bfloat16))
    for w in range(TERMS):
        total = jnp.zeros((size, size), jnp.float32)
        for t in range(slots):
            block = first_env[owner[0, t], w * size : (w + 1) * size]
            done = jnp.dot(block, rounded[t], preferred_element_type=jnp.float32).astype(jnp.bfloat16)
            total = total + lax.dot_general(
                rounded[t], done, (((0,), (0,)), ((), ())), preferred_element_type=jnp.float32
            )
        fresh[w * size : (w + 1) * size] = (states * total).astype(jnp.bfloat16)

        @pl.when(has_next)
        def _(w=w):
            onward[w].start()

    @pl.when(has_previous)
    def _():
        for copy in gather(2, second_env, lambda w: onward[w].wait_recv()):
            copy.wait_send()

    @pl.when(jnp.logical_not(has_previous))
    def _():
        pltpu.make_async_copy(first_env, second_env, local_sems.at[3]).wait()

    weights, second_ritz, second_sums = krylov(3, second_env, lambda t, q, m: field[0, t])

    for t in range(slots):
        field[0, t] = states * combined(t, weights[t])
    for q in range(count):
        waves_ref[q] = jnp.where(matches[q], field[0, jnp.minimum(places[q], slots - 1)], 0.0)
    lane = lax.broadcasted_iota(jnp.int32, (1, size), 1)
    energies_ref[...] = jnp.where(lane == 0, first_ritz, second_ritz)[:, :2]

    for copies in (first_copies, first_sums.values(), second_sums.values()):
        for copy in copies:
            copy.wait_send()

    @pl.when(has_next)
    def _():
        for copy in onward:
            copy.wait_send()


def solution(mesh):
    count = mesh.shape["blk"]
    sections = mesh.shape["sec"]

    def local(guess, left_env, right_env, left_dims, right_dims, left_labels, right_labels):
        size = guess.shape[2]
        terms = left_env.shape[1]
        rows = terms * size
        smem = pl.BlockSpec(memory_space=pltpu.SMEM)
        anywhere = pl.BlockSpec(memory_space=pltpu.HBM)
        vmem = pl.BlockSpec(memory_space=pltpu.VMEM)
        moments = 2 * ITERS + 2
        waves, energies = pl.pallas_call(
            functools.partial(kernel, count, sections, size, moments),
            out_shape=(
                pltpu.VMEM((count, size, size), jnp.float32),
                pltpu.VMEM((1, 2), jnp.float32),
            ),
            in_specs=[smem] * 4 + [anywhere] * 3,
            out_specs=(vmem, vmem),
            scratch_shapes=[
                pltpu.VMEM((count, size, size), jnp.bfloat16),
                pltpu.VMEM((rows, size), jnp.bfloat16),
                pltpu.VMEM((count, rows, size), jnp.bfloat16),
                pltpu.VMEM((count, rows, size), jnp.bfloat16),
                pltpu.VMEM((3, count - TOTAL, size, size), jnp.float32),
                pltpu.VMEM((count - TOTAL, 8, size), jnp.float32),
                pltpu.VMEM((rows, size), jnp.bfloat16),
                pltpu.VMEM((2, count, 8, size), jnp.float32),
                pltpu.SMEM((2, count), jnp.int32),
                pltpu.SemaphoreType.DMA((4,)),
                pltpu.SemaphoreType.DMA((4, count, TERMS)),
                pltpu.SemaphoreType.DMA((4, count, TERMS)),
                pltpu.SemaphoreType.DMA((2, TERMS)),
            ],
            compiler_params=pltpu.CompilerParams(
                collective_id=0, has_side_effects=True, vmem_limit_bytes=64 * 1024 * 1024 - 10 * count * size * size
            ),
        )(
            left_dims, right_dims, left_labels, right_labels,
            guess.reshape(count, size, size), left_env.reshape(rows, size), right_env.reshape(rows, size),
        )
        return waves.reshape(1, count, size, 1, size), energies

    return jax.shard_map(
        local,
        mesh=mesh,
        in_specs=(
            P("sec", None, None, "blk", None),
            P("sec", None, "blk", None, None),
            P("sec", None, "blk", None, None),
            P("sec", None),
            P("sec", None),
            P("sec", None),
            P("sec", None),
        ),
        out_specs=(P("sec", None, None, "blk", None), P("sec", None)),
        check_vma=False,
    )
```

```python
import functools

import jax
import jax.numpy as jnp
from jax import lax
from jax.experimental import pallas as pl
from jax.experimental.pallas import tpu as pltpu
from jax.sharding import PartitionSpec as P

MESH = pl.DeviceIdType.MESH
ITERS = 2
EPS = 1e-06
SPAN = 32.0
FLOOR = 1e-12
GROUP = 4
TOTAL = 4
TERMS = 2


def target(me, offset, count):
    chip = lax.rem(lax.div(me, 2) + offset // 2, count // 2)
    return chip * 2 + lax.rem(me + offset, 2)


def origin(me, offset, count):
    chip = lax.rem(lax.div(me, 2) + count // 2 - offset // 2, count // 2)
    return chip * 2 + lax.rem(me + offset, 2)


def polynomial(mu, floor_squared):
    zero = jnp.zeros_like(mu[0])
    vector = [zero + 1.0]
    image = [zero, zero + 1.0]
    ritz = mu[1]
    for _ in range(ITERS):
        padded = vector + [zero]
        residual = [image[i] - ritz * padded[i] for i in range(len(image))]
        size = len(residual)
        squared = zero
        correlation = zero
        for i in range(size):
            for j in range(size):
                weight = residual[i] * residual[j]
                squared = squared + weight * mu[i + j]
                correlation = correlation + weight * mu[i + j + 1]
        squared = jnp.maximum(squared, 0.0) + floor_squared
        coupling = correlation / squared
        midpoint = 0.5 * (ritz - coupling)
        radius = jnp.sqrt(midpoint * midpoint + squared)
        cosine = jnp.sqrt(0.5 * (1.0 - midpoint / radius))
        sine = -jnp.sqrt(0.5 * (1.0 + midpoint / radius))
        tilt = sine / jnp.sqrt(squared)
        vector = [cosine * padded[i] + tilt * residual[i] for i in range(size)]
        image = [zero] + vector
        ritz = 0.5 * (ritz + coupling) - radius
    return vector, ritz


def kernel(
    count, sections, size, moments,
    left_dims, right_dims, left_labels, right_labels, guess_ref, left_ref, right_ref,
    waves_ref, energies_ref,
    guess, right, first_env, second_env, field, stats, fresh, sums, owner,
    local_sems, send_sems, recv_sems, pass_sems,
):
    sec = lax.axis_index("sec")
    me = lax.axis_index("blk")
    states = count * size
    slots = count - TOTAL
    has_next = sec < sections - 1
    has_previous = sec > 0

    load_left = pltpu.make_async_copy(left_ref, first_env.at[me], local_sems.at[1])
    load_guess = pltpu.make_async_copy(guess_ref, guess, local_sems.at[2])
    load_right = pltpu.make_async_copy(right_ref, right, local_sems.at[0])
    load_left.start()
    load_guess.start()
    load_right.start()

    barrier = pltpu.get_barrier_semaphore()
    for k in range(1, count):
        pl.semaphore_signal(barrier, inc=1, device_id=(sec, target(me, k, count)), device_id_type=MESH)

    @pl.when(has_next)
    def _():
        pl.semaphore_signal(barrier, inc=1, device_id=(sec + 1, me), device_id_type=MESH)

    @pl.when(has_previous)
    def _():
        pl.semaphore_signal(barrier, inc=1, device_id=(sec - 1, me), device_id_type=MESH)

    mark = right_labels[0, me]
    places = []
    seen = jnp.int32(0)
    matches = []
    for q in range(count):
        match = left_labels[0, q] + mark == TOTAL
        places.append(seen)
        matches.append(match)
        seen = seen + match.astype(jnp.int32)
    for t in range(slots):
        sector = jnp.int32(0)
        dims = jnp.int32(0)
        for q in range(count):
            here = jnp.logical_and(matches[q], places[q] == t)
            sector = jnp.where(here, q, sector)
            dims = jnp.where(here, left_dims[0, q], dims)
        owner[0, t] = sector
        owner[1, t] = dims

    load_left.wait()
    pl.semaphore_wait(barrier, count - 1 + has_next.astype(jnp.int32) + has_previous.astype(jnp.int32))

    def copy_to(phase, k, hop, source, slot, part=0):
        return pltpu.make_async_remote_copy(
            src_ref=source,
            dst_ref=slot,
            send_sem=send_sems.at[phase, k, part],
            recv_sem=recv_sems.at[phase, k, part],
            device_id=(sec, target(me, hop, count)),
            device_id_type=MESH,
        )

    def term(ref, w):
        return ref.at[pl.ds(w * size, size)]

    def routes(phase, env):
        copies = {}
        for w in range(TERMS):
            block = term(env.at[me], w)
            for k in list(range(count - 2, 0, -2)) + [1]:
                copies[k, w] = copy_to(phase, k, k, block, block, w)
            for k in range(2, count, 2):
                block = term(env.at[origin(me, k, count)], w)
                copies[k + 1, w] = copy_to(phase, k + 1, 1, block, block, w)
        return copies

    def gather(copies, arrive):
        for w in range(TERMS):
            arrive(w)
            for k in list(range(count - 2, 0, -2)) + [1]:
                copies[k, w].start()
        for w in range(TERMS):
            for k in range(2, count, 2):
                copies[k, w].wait_recv()
                copies[k + 1, w].start()
        for w in range(TERMS):
            for k in range(1, count, 2):
                copies[k, w].wait_recv()

    first_copies = routes(0, first_env)
    second_copies = routes(2, second_env)
    gather(first_copies, lambda w: None)

    @pl.when(jnp.logical_not(has_previous))
    def _():
        pltpu.make_async_copy(first_env, second_env, local_sems.at[3]).start()

    rows = lax.broadcasted_iota(jnp.int32, (size, size), 0)
    cols = lax.broadcasted_iota(jnp.int32, (size, size), 1)
    live_cols = cols < right_dims[0, me]

    load_guess.wait()
    load_right.wait()
    right_all = right[...]
    right_peak = jnp.max(jnp.abs(right_all.astype(jnp.float32)), axis=(0, 1), keepdims=True) * SPAN

    def folded(values):
        return jnp.sum(values.reshape(-1, 8, size), axis=0)

    def chain(env, ts, start):
        sectors = [owner[0, t] for t in ts]
        blocks = [env[q] for q in sectors]
        masks = [jnp.logical_and(rows < owner[1, t], live_cols) for t in ts]
        scales = [
            jnp.maximum(jnp.max(jnp.abs(b.astype(jnp.float32)), axis=(0, 1), keepdims=True) * right_peak, FLOOR)
            for b in blocks
        ]
        inverse = [1.0 / s for s in scales]
        powers = [[start(t, q, m) for t, q, m in zip(ts, sectors, masks)]]
        for _ in range(3):
            lefts = [
                jnp.dot(b, v.astype(jnp.bfloat16), preferred_element_type=jnp.float32).astype(jnp.bfloat16)
                for b, v in zip(blocks, powers[-1])
            ]
            lefts = [jnp.concatenate([x[:size], x[size:]], axis=1) for x in lefts]
            full = jnp.dot(jnp.concatenate(lefts, axis=0), right_all, preferred_element_type=jnp.float32)
            powers.append([
                jnp.where(m, full[at * size : (at + 1) * size] * i, 0.0)
                for at, (m, i) in enumerate(zip(masks, inverse))
            ])
        for at, t in enumerate(ts):
            kept = [p[at] for p in powers]
            for i in range(3):
                field[i, t] = kept[i]
            line = [
                jnp.sum(folded(kept[i // 2] * kept[(i + 1) // 2]), axis=0, keepdims=True) for i in range(moments)
            ]
            line.append(jnp.broadcast_to(scales[at], (1, size)))
            line.append(jnp.zeros((1, size), jnp.float32))
            stats[t] = jnp.concatenate(line, axis=0)

    index = lax.broadcasted_iota(jnp.int32, (8, size), 0)

    def merged(tiles):
        peaks = [tile[moments : moments + 1] for tile in tiles]
        top = functools.reduce(jnp.maximum, peaks)
        total = jnp.zeros((8, size), jnp.float32)
        for tile, peak in zip(tiles, peaks):
            ratio = peak / top
            power = ratio
            weight = jnp.ones((8, size), jnp.float32)
            for i in range(1, moments):
                weight = jnp.where(index == i, power, weight)
                power = power * ratio
            total = total + tile * weight
        return jnp.where(index == moments, top, total), top

    def krylov(phase, env, start):
        if slots % GROUP == 0 and slots > GROUP:

            def step(g, carry):
                chain(env, [g * GROUP + i for i in range(GROUP)], start)
                return carry

            lax.fori_loop(0, slots // GROUP, step, 0)
        else:
            for first in range(0, slots, GROUP):
                chain(env, list(range(first, min(first + GROUP, slots))), start)
        row = phase // 2
        tiles = [stats[t] for t in range(slots)]
        sums[row, me] = merged(tiles)[0]
        copies = {k: copy_to(phase, k, k, sums.at[row, me], sums.at[row, me]) for k in range(1, count)}
        for k in copies:
            copies[k].start()
        for k in copies:
            copies[k].wait_recv()
        total, top = merged([sums[row, j] for j in range(count)])
        summed = jnp.broadcast_to(jnp.sum(total, axis=1, keepdims=True), (8, size))
        mu = [summed[i : i + 1] for i in range(moments)]
        norm = mu[0] + EPS
        mu = [m / norm for m in mu]
        relative = EPS**0.5 / top
        vector, ritz = polynomial(mu, relative * relative)
        shrink = lax.rsqrt(norm)
        weights = []
        for tile in tiles:
            ratio = tile[moments : moments + 1] / top
            weights.append([vector[0] * shrink, vector[1] * shrink * ratio, vector[2] * shrink * ratio * ratio])
        return weights, ritz * top, copies

    def combined(t, weight):
        return weight[0] * field[0, t] + weight[1] * field[1, t] + weight[2] * field[2, t]

    weights, first_ritz, first_sums = krylov(
        1, first_env, lambda t, q, m: jnp.where(m, guess[q].astype(jnp.float32), 0.0)
    )

    onward = [
        pltpu.make_async_remote_copy(
            src_ref=term(fresh, w),
            dst_ref=term(second_env.at[me], w),
            send_sem=pass_sems.at[0, w],
            recv_sem=pass_sems.at[1, w],
            device_id=(lax.rem(sec + 1, sections), me),
            device_id_type=MESH,
        )
        for w in range(TERMS)
    ]
    rounded = []
    for t in range(slots):
        vector = combined(t, weights[t])
        field[0, t] = vector
        rounded.append(vector.astype(jnp.bfloat16))
    for w in range(TERMS):
        total = jnp.zeros((size, size), jnp.float32)
        for t in range(slots):
            block = first_env[owner[0, t], w * size : (w + 1) * size]
            done = jnp.dot(block, rounded[t], preferred_element_type=jnp.float32).astype(jnp.bfloat16)
            total = total + lax.dot_general(
                rounded[t], done, (((0,), (0,)), ((), ())), preferred_element_type=jnp.float32
            )
        fresh[w * size : (w + 1) * size] = (states * total).astype(jnp.bfloat16)

        @pl.when(has_next)
        def _(w=w):
            onward[w].start()

    @pl.when(has_previous)
    def _():
        gather(second_copies, lambda w: onward[w].wait_recv())

    @pl.when(jnp.logical_not(has_previous))
    def _():
        pltpu.make_async_copy(first_env, second_env, local_sems.at[3]).wait()

    weights, second_ritz, second_sums = krylov(3, second_env, lambda t, q, m: field[0, t])

    for t in range(slots):
        field[0, t] = states * combined(t, weights[t])
    for q in range(count):
        waves_ref[q] = jnp.where(matches[q], field[0, jnp.minimum(places[q], slots - 1)], 0.0)
    lane = lax.broadcasted_iota(jnp.int32, (1, size), 1)
    energies_ref[...] = jnp.where(lane == 0, first_ritz, second_ritz)[:, :2]

    for copies in (first_copies.values(), first_sums.values(), second_sums.values()):
        for copy in copies:
            copy.wait_send()

    @pl.when(has_previous)
    def _():
        for copy in second_copies.values():
            copy.wait_send()

    @pl.when(has_next)
    def _():
        for copy in onward:
            copy.wait_send()


def solution(mesh):
    count = mesh.shape["blk"]
    sections = mesh.shape["sec"]

    def local(guess, left_env, right_env, left_dims, right_dims, left_labels, right_labels):
        size = guess.shape[2]
        terms = left_env.shape[1]
        rows = terms * size
        smem = pl.BlockSpec(memory_space=pltpu.SMEM)
        anywhere = pl.BlockSpec(memory_space=pltpu.HBM)
        vmem = pl.BlockSpec(memory_space=pltpu.VMEM)
        moments = 2 * ITERS + 2
        waves, energies = pl.pallas_call(
            functools.partial(kernel, count, sections, size, moments),
            out_shape=(
                pltpu.VMEM((count, size, size), jnp.float32),
                pltpu.VMEM((1, 2), jnp.float32),
            ),
            in_specs=[smem] * 4 + [anywhere] * 3,
            out_specs=(vmem, vmem),
            scratch_shapes=[
                pltpu.VMEM((count, size, size), jnp.bfloat16),
                pltpu.VMEM((rows, size), jnp.bfloat16),
                pltpu.VMEM((count, rows, size), jnp.bfloat16),
                pltpu.VMEM((count, rows, size), jnp.bfloat16),
                pltpu.VMEM((3, count - TOTAL, size, size), jnp.float32),
                pltpu.VMEM((count - TOTAL, 8, size), jnp.float32),
                pltpu.VMEM((rows, size), jnp.bfloat16),
                pltpu.VMEM((2, count, 8, size), jnp.float32),
                pltpu.SMEM((2, count), jnp.int32),
                pltpu.SemaphoreType.DMA((4,)),
                pltpu.SemaphoreType.DMA((4, count, TERMS)),
                pltpu.SemaphoreType.DMA((4, count, TERMS)),
                pltpu.SemaphoreType.DMA((2, TERMS)),
            ],
            compiler_params=pltpu.CompilerParams(
                collective_id=0, has_side_effects=True, vmem_limit_bytes=64 * 1024 * 1024 - 10 * count * size * size
            ),
        )(
            left_dims, right_dims, left_labels, right_labels,
            guess.reshape(count, size, size), left_env.reshape(rows, size), right_env.reshape(rows, size),
        )
        return waves.reshape(1, count, size, 1, size), energies

    return jax.shard_map(
        local,
        mesh=mesh,
        in_specs=(
            P("sec", None, None, "blk", None),
            P("sec", None, "blk", None, None),
            P("sec", None, "blk", None, None),
            P("sec", None),
            P("sec", None),
            P("sec", None),
            P("sec", None),
        ),
        out_specs=(P("sec", None, None, "blk", None), P("sec", None)),
        check_vma=False,
    )
```
